32 devices in a mesh: seq: 4 (over y, x), head: 4 (over z), fsdp: 2 (over core).
Axes of the slice: x: 2, y: 2, z: 4, core: 2. Of those that a mesh axis runs over, the one named last changes fastest.
Arguments:
- query: bfloat16 [2, 512, 1024], P('fsdp', 'seq', 'head'), may hold values from -6 to 6
- keys: bfloat16 [2, 512, 1024], P('fsdp', 'seq', 'head'), may hold values from -6 to 6
- values: bfloat16 [2, 512, 1024], P('fsdp', 'seq', 'head'), may hold values from -6 to 6
- grad_out: bfloat16 [2, 512, 4096], P('fsdp', 'seq'), may hold values from -6 to 6
- w_out: bfloat16 [1024, 4096], P('head', 'fsdp'), may hold values from -0.1875 to 0.1875
- link_flags: int32 [4, 2], P('seq'), may hold values 0 or 1
Outputs:
- grad_query: bfloat16 [2, 512, 1024], P('fsdp', 'seq', 'head')
- grad_keys: bfloat16 [2, 512, 1024], P('fsdp', 'seq', 'head')
- grad_values: bfloat16 [2, 512, 1024], P('fsdp', 'seq', 'head')
- grad_w_out_t: float32 [4096, 1024], P('seq', ('head', 'fsdp'))
The draws below stay inside these ranges and needn't reach their ends.
All inputs are finite; a program needn't handle non-finite values. No bound on the sum of `link_flags` on one device may be relied on, other than what follows from the above.
Results may differ from the reference program's by a relative error of at most 0.01.
Values may be sent and summed in bfloat16 or wider, within the bound.
A program may use at most 64 MiB of HBM per device.

```python
import math
import jax
import jax.numpy as jnp
from jax import lax

D = 4096
HD = 128
BLK = 128
HEADS = 8
SEQ_BITS = 2
SEQLEN = 512
BATCH = 2
N_SEQ = 4


def query_key_pair(key):
    query_key = jax.random.fold_in(key, 11)
    keys_key = jax.random.fold_in(key, 12)
    shape = (BATCH, SEQLEN, HEADS * HD)
    queries = jnp.clip(jax.random.normal(query_key, shape, jnp.float32), -6.0, 6.0)
    keyset = jnp.clip(jax.random.normal(keys_key, shape, jnp.float32), -6.0, 6.0)
    return (queries.astype(jnp.bfloat16), keyset.astype(jnp.bfloat16))


def draw_query(key, part):
    return query_key_pair(key)[0]


def draw_keys(key, part):
    return query_key_pair(key)[1]


def touch_ends(values, stream_key, low, largest):
    shape = values.shape
    index_at = [jax.random.randint(jax.random.fold_in(stream_key, axis), (), 0, shape[axis]) for axis in range(len(shape))]
    values = values.at[tuple(index_at)].set(low)
    longest = shape.index(max(shape))
    index_at[longest] = (index_at[longest] + 1) % shape[longest]
    return values.at[tuple(index_at)].set(largest)


def raised(entries, own_key, source, target, parts, factor):
    def block_of(axis_at):
        return (jnp.arange(entries.shape[axis_at]) // (entries.shape[axis_at] // parts)).reshape((-1,) + (1,) * (entries.ndim - 1 - axis_at))

    first = jax.random.permutation(own_key, parts)[block_of(target)]
    far = (block_of(target) + parts // 2) % parts
    return jnp.where((block_of(source) == first) | (block_of(source) == far), factor * entries, entries)


def steps_of(key, dims, split, smallest, high):
    def one(position, parts):
        draws = jax.random.uniform(jax.random.fold_in(jax.random.fold_in(key, 6), position), (parts,), jnp.float32, smallest / len(split), high / len(split))
        return jnp.repeat(jnp.exp(draws), dims[position] // parts).reshape((-1,) + (1,) * (len(dims) - position - 1))

    loudness = one(*split[0])
    for cut in split[1:]:
        loudness = loudness * one(*cut)
    return loudness


def scatter_about(own_key, shape, spread, reach, pieces=(), kind=jnp.bfloat16):
    result = jax.random.normal(own_key, shape, jnp.float32) * spread
    if len(pieces) > 0:
        result = steps_of(own_key, shape, pieces, -0.22, 0.18) * result
    return jnp.clip(result, min=-reach, max=reach).astype(kind)


def heavy_noise(own_key, extent, spread, most, split, heavy, held_as=jnp.bfloat16):
    values = spread * jax.random.normal(own_key, extent, jnp.float32)
    if split:
        values = values * steps_of(own_key, extent, split, -0.22, 0.18)
    return jnp.clip(raised(values, jax.random.fold_in(own_key, 3), *heavy), -most, most).astype(held_as)


def setup_inputs(seed: int = 0) -> dict:
    key_of = jax.random.split(jax.random.key(seed), 7)
    return {
        "query": draw_query(jax.random.fold_in(key_of[6], 71), 0),
        "keys": draw_keys(jax.random.fold_in(key_of[6], 71), 0),
        "values": scatter_about(key_of[2], (BATCH, SEQLEN, HEADS * HD), 1.0, 6.0, ((0, 2), (1, 4), (2, 4))),
        "grad_out": heavy_noise(key_of[3], (BATCH, SEQLEN, D), 1.0, 6.0, ((0, 2), (1, 4)), (1, 2, 4, 2.0)),
        "w_out": scatter_about(key_of[4], (HEADS * HD, D), (HEADS * HD) ** -0.5, 0.1875, ((0, 4), (1, 2))),
        "link_flags": touch_ends((jax.random.randint(key_of[5], (N_SEQ, SEQ_BITS), 0, 4) < 3).astype(jnp.int32), jax.random.fold_in(key_of[5], 1), 0, 1),
    }


def split_heads(array, nblocks):
    shaped = array.reshape(BATCH, nblocks, BLK, HEADS, HD).transpose(0, 3, 1, 2, 4)
    return shaped.reshape(BATCH * HEADS, nblocks, BLK, HD)

def merge_heads(array, nblocks):
    shaped = array.reshape(BATCH, HEADS, nblocks, BLK, HD).transpose(0, 2, 3, 1, 4)
    return shaped.reshape(BATCH, nblocks * BLK, HEADS * HD)

def reference(query, keys, values, grad_out, w_out, link_flags):
    score_scale = 1.0 / math.sqrt(HD)
    nblocks = N_SEQ
    levels = SEQ_BITS
    base = jnp.arange(nblocks, dtype=jnp.int32)
    partner = jnp.stack([base] + [jnp.bitwise_xor(base, 2 ** level).astype(jnp.int32) for level in range(levels)], axis=1)
    spots = jnp.arange(BLK, dtype=jnp.int32)
    causal = spots[None, :] <= spots[:, None]
    link_on = jnp.concatenate([jnp.ones((nblocks, 1), dtype=bool), link_flags > 0], axis=1)
    first_slot = jnp.arange(levels + 1, dtype=jnp.int32) == 0
    allowed = jnp.where(first_slot[None, None, :, None], causal[None, :, None, :], link_on[:, None, :, None])
    grad_rows = grad_out.reshape(BATCH * SEQLEN, D)
    grad_att = jnp.dot(grad_rows, w_out.T, preferred_element_type=jnp.float32).astype(jnp.bfloat16)
    stacked = (split_heads(query, nblocks), split_heads(keys, nblocks), split_heads(values, nblocks), split_heads(grad_att.reshape(BATCH, SEQLEN, HEADS * HD), nblocks))

    def one_head(operands):
        query_blocks, key_blocks, value_blocks, grad_blocks = operands
        query_wide = query_blocks.astype(jnp.float32)
        grad_wide = grad_blocks.astype(jnp.float32)
        key_near = key_blocks[partner].astype(jnp.float32)
        value_near = value_blocks[partner].astype(jnp.float32)
        scores = jnp.einsum('itc,imuc->itmu', query_wide, key_near) * score_scale
        scores = jnp.where(allowed, scores, -jnp.inf)
        row_max = lax.optimization_barrier(jnp.max(scores, axis=(2, 3), keepdims=True))
        raw = jnp.exp(scores - row_max)
        softmax = raw / lax.optimization_barrier(jnp.sum(raw, axis=(2, 3), keepdims=True))
        probs_low = softmax.astype(jnp.bfloat16)
        attended = jnp.einsum('itmu,imuc->itc', probs_low.astype(jnp.float32), value_near).astype(jnp.bfloat16)
        grad_probs = jnp.einsum('itc,imuc->itmu', grad_wide, value_near)
        row_dot = lax.optimization_barrier(jnp.sum(softmax * grad_probs, axis=(2, 3), keepdims=True))
        grad_scores = (softmax * (grad_probs - row_dot) * score_scale).astype(jnp.bfloat16)
        grad_query = jnp.einsum('itmu,imuc->itc', grad_scores.astype(jnp.float32), key_near).astype(jnp.bfloat16)
        key_terms = jnp.einsum('itmu,itc->imuc', grad_scores.astype(jnp.float32), query_wide)
        value_terms = jnp.einsum('itmu,itc->imuc', probs_low.astype(jnp.float32), grad_wide)
        grad_key = key_terms[:, 0]
        grad_value = value_terms[:, 0]
        for level in range(levels):
            key_low = lax.optimization_barrier(key_terms[:, level + 1].astype(jnp.bfloat16)).astype(jnp.float32)
            value_low = lax.optimization_barrier(value_terms[:, level + 1].astype(jnp.bfloat16)).astype(jnp.float32)
            grad_key = grad_key + key_low[partner[:, level + 1]]
            grad_value = grad_value + value_low[partner[:, level + 1]]
        return (attended, grad_query, grad_key.astype(jnp.bfloat16), grad_value.astype(jnp.bfloat16))
    results = lax.map(one_head, stacked)
    attended = merge_heads(results[0], nblocks)
    grad_w = jnp.dot(grad_rows.T, attended.reshape(BATCH * SEQLEN, HEADS * HD), preferred_element_type=jnp.float32)
    return (merge_heads(results[1], nblocks), merge_heads(results[2], nblocks), merge_heads(results[3], nblocks), grad_w)
```

```python
import functools
import math

import jax
import jax.numpy as jnp
from jax import lax
from jax.experimental import pallas as pl
from jax.experimental.pallas import tpu as pltpu
from jax.sharding import PartitionSpec as P

D = 4096
HD = 128


def swapped(shard, axis, distance):
    return lax.ppermute(shard, axis, [(i, i ^ 1 << distance) for i in range(lax.axis_size(axis))])


def plain_device(query, keys, values, grad_out, w_out, link_flags):
    local_seqs, block_len, local_width = query.shape
    local_heads = local_width // HD
    levels = lax.axis_size("seq").bit_length() - 1
    score_scale = 1.0 / math.sqrt(HD)
    key_value = jnp.stack([keys, values])
    collected = [key_value]
    for level in range(levels):
        collected.append(swapped(key_value, "seq", level))
    slots = levels + 1
    near_all = jnp.stack(collected).reshape(slots, 2, local_seqs, block_len, local_heads, HD)
    key_near = near_all[:, 0]
    value_near = near_all[:, 1]
    query_heads = query.reshape(local_seqs, block_len, local_heads, HD)
    spots = jnp.arange(block_len, dtype=jnp.int32)
    causal = spots[None, :] <= spots[:, None]
    link_on = jnp.concatenate([jnp.ones((1,), dtype=bool), link_flags[0] > 0])
    first_slot = jnp.arange(slots, dtype=jnp.int32) == 0
    allowed = jnp.where(first_slot[None, :, None], causal[:, None, :], link_on[None, :, None])
    scores = (
        jnp.einsum("sthc,msuhc->shtmu", query_heads, key_near, preferred_element_type=jnp.float32)
        * score_scale
    )
    scores = jnp.where(allowed[None, None], scores, -jnp.inf)
    row_max = jnp.max(scores, axis=(3, 4), keepdims=True)
    raw = jnp.exp(scores - row_max)
    softmax = raw / jnp.sum(raw, axis=(3, 4), keepdims=True)
    probs_low = softmax.astype(jnp.bfloat16)
    attended = jnp.einsum(
        "shtmu,msuhc->sthc", probs_low, value_near, preferred_element_type=jnp.float32
    ).astype(jnp.bfloat16)
    grad_rows = grad_out.reshape(local_seqs * block_len, D)
    columns = grad_rows
    grad_att = lax.dot_general(
        columns,
        lax.all_gather(w_out, "fsdp", axis=1, tiled=True),
        (((1,), (1,)), ((), ())),
        preferred_element_type=jnp.float32,
    ).astype(jnp.bfloat16)
    grad_heads = grad_att.reshape(local_seqs, block_len, local_heads, HD)
    attended_rows = attended.reshape(local_seqs * block_len, local_width)
    columns = grad_rows
    seq_share = lax.psum_scatter(
        lax.dot_general(
            columns, attended_rows, (((0,), (0,)), ((), ())), preferred_element_type=jnp.float32
        ),
        "seq",
        scatter_dimension=0,
        tiled=True,
    )
    grad_w = lax.psum_scatter(
        seq_share.astype(jnp.bfloat16), "fsdp", scatter_dimension=1, tiled=True
    ).astype(jnp.float32)
    grad_probs = jnp.einsum(
        "sthc,msuhc->shtmu", grad_heads, value_near, preferred_element_type=jnp.float32
    )
    row_dot = jnp.sum(softmax * grad_probs, axis=(3, 4), keepdims=True)
    grad_scores = (softmax * (grad_probs - row_dot) * score_scale).astype(jnp.bfloat16)
    grad_query = jnp.einsum(
        "shtmu,msuhc->sthc", grad_scores, key_near, preferred_element_type=jnp.float32
    ).astype(jnp.bfloat16)
    key_terms = jnp.einsum(
        "shtmu,sthc->msuhc", grad_scores, query_heads, preferred_element_type=jnp.float32
    )
    value_terms = jnp.einsum(
        "shtmu,sthc->msuhc", probs_low, grad_heads, preferred_element_type=jnp.float32
    )
    grad_key = key_terms[0]
    grad_value = value_terms[0]
    for level in range(levels):
        outgoing = jnp.stack([key_terms[level + 1], value_terms[level + 1]]).astype(jnp.bfloat16)
        returned = swapped(outgoing, "seq", level)
        grad_key = grad_key + returned[0].astype(jnp.float32)
        grad_value = grad_value + returned[1].astype(jnp.float32)
    shape_out = (local_seqs, block_len, local_width)
    return (
        grad_query.reshape(shape_out),
        grad_key.astype(jnp.bfloat16).reshape(shape_out),
        grad_value.astype(jnp.bfloat16).reshape(shape_out),
        grad_w,
    )


def contract(a, b, dims):
    return lax.dot_general(a, b, (dims, ((), ())), preferred_element_type=jnp.float32)


def fused_kernel(
    n_seq,
    flags_ref,
    query_hbm,
    keys_hbm,
    values_hbm,
    go_hbm,
    w_hbm,
    gq_ref,
    gk_ref,
    gv_ref,
    gw_ref,
    q_buf,
    k_all,
    v_all,
    go_buf,
    w_all,
    go_all,
    att_all,
    term_send,
    term_recv,
    gk_acc,
    gv_acc,
    part_send,
    part_recv,
    local_sem,
    kv_send_sem,
    kv_recv_sem,
    w_sem,
    go_send_sem,
    go_recv_sem,
    att_send_sem,
    att_recv_sem,
    term_send_sem,
    term_recv_sem,
    part_send_sem,
    part_recv_sem,
):
    levels = n_seq.bit_length() - 1
    block, width = q_buf.shape
    heads = width // HD
    rows = go_all.shape[1]
    half_d = w_hbm.shape[1]
    half_w = width // 2
    scale = 1.0 / math.sqrt(HD)
    me = lax.axis_index("seq")
    core = lax.axis_index("fsdp")
    other = 1 - core

    def peer(mask):
        out = me
        for bit in range(levels):
            if mask >> bit & 1:
                out = out + (1 << bit) * (1 - 2 * (lax.div(me, 1 << bit) % 2))
        return out

    def remote(src, dst, send, recv, target):
        return pltpu.make_async_remote_copy(
            src_ref=src,
            dst_ref=dst,
            send_sem=send,
            recv_sem=recv,
            device_id=target,
            device_id_type=pl.DeviceIdType.MESH,
        )

    locals_ = [
        pltpu.make_async_copy(query_hbm, q_buf, local_sem.at[0]),
        pltpu.make_async_copy(keys_hbm, k_all.at[pl.ds(0, block)], local_sem.at[1]),
        pltpu.make_async_copy(values_hbm, v_all.at[pl.ds(0, block)], local_sem.at[2]),
        pltpu.make_async_copy(go_hbm, go_buf, local_sem.at[3]),
        pltpu.make_async_copy(w_hbm, w_all.at[0], local_sem.at[4]),
    ]
    for copy in locals_:
        copy.start()

    barrier = pltpu.get_barrier_semaphore()
    for mask in range(1, n_seq):
        pl.semaphore_signal(
            barrier, inc=1, device_id={"seq": peer(mask)}, device_id_type=pl.DeviceIdType.MESH
        )
    pl.semaphore_signal(
        barrier, inc=1, device_id={"fsdp": other}, device_id_type=pl.DeviceIdType.MESH
    )
    pl.semaphore_wait(barrier, n_seq)

    kv_copies = []
    for level in range(levels):
        spot = pl.ds((level + 1) * block, block)
        for which, (src, dst) in enumerate(((keys_hbm, k_all), (values_hbm, v_all))):
            i = 2 * level + which
            kv_copies.append(
                remote(
                    src,
                    dst.at[spot],
                    kv_send_sem.at[i],
                    kv_recv_sem.at[i],
                    {"seq": peer(1 << level)},
                )
            )
    for copy in kv_copies:
        copy.start()
    w_copy = remote(w_hbm, w_all.at[1], w_sem.at[0], w_sem.at[1], {"fsdp": other})
    w_copy.start()
    go_copies = []
    for mask in range(1, n_seq):
        target = peer(mask)
        columns = pl.ds(pl.multiple_of(target * rows, 128), rows)
        go_copies.append(
            remote(
                go_hbm.at[:, columns],
                go_all.at[pl.ds(mask * block, block)],
                go_send_sem.at[mask - 1],
                go_recv_sem.at[mask - 1],
                {"seq": target},
            )
        )
    for copy in go_copies:
        copy.start()

    locals_[3].wait()
    locals_[4].wait()
    own_columns = pl.ds(pl.multiple_of(core * half_d, 128), half_d)
    other_columns = pl.ds(pl.multiple_of(other * half_d, 128), half_d)
    grad_att = contract(go_buf[:, own_columns], w_all[0], ((1,), (1,)))
    go_all[pl.ds(0, block), :] = go_buf[:, pl.ds(pl.multiple_of(me * rows, 128), rows)]

    for copy in locals_[:3]:
        copy.wait()
    for copy in kv_copies:
        copy.wait_recv()

    spots_t = lax.broadcasted_iota(jnp.int32, (block, block), 0)
    spots_u = lax.broadcasted_iota(jnp.int32, (block, block), 1)
    allowed = [spots_u <= spots_t]
    for level in range(levels):
        allowed.append(jnp.full((block, block), flags_ref[0, level], jnp.int32) > 0)
    allowed = jnp.concatenate(allowed, axis=1)

    softmaxes = []
    lows = []
    for h in range(heads):
        cols = slice(h * HD, (h + 1) * HD)
        scores = contract(q_buf[:, cols], k_all[:, cols], ((1,), (1,))) * scale
        scores = jnp.where(allowed, scores, -jnp.inf)
        raw = jnp.exp(scores - jnp.max(scores, axis=1, keepdims=True))
        softmax = raw / jnp.sum(raw, axis=1, keepdims=True)
        low = softmax.astype(jnp.bfloat16)
        att_all[pl.ds(0, block), cols] = contract(low, v_all[:, cols], ((1,), (0,))).astype(
            jnp.bfloat16
        )
        softmaxes.append(softmax)
        lows.append(low)

    att_copies = []
    for mask in range(1, n_seq):
        att_copies.append(
            remote(
                att_all.at[pl.ds(0, block)],
                att_all.at[pl.ds(mask * block, block)],
                att_send_sem.at[mask - 1],
                att_recv_sem.at[mask - 1],
                {"seq": peer(mask)},
            )
        )
    for copy in att_copies:
        copy.start()

    w_copy.wait_recv()
    grad_att = grad_att + contract(go_buf[:, other_columns], w_all[1], ((1,), (1,)))
    grad_att = grad_att.astype(jnp.bfloat16)

    for h in range(heads):
        cols = slice(h * HD, (h + 1) * HD)
        grad_head = grad_att[:, cols]
        grad_probs = contract(grad_head, v_all[:, cols], ((1,), (1,)))
        row_dot = jnp.sum(softmaxes[h] * grad_probs, axis=1, keepdims=True)
        grad_scores = (softmaxes[h] * (grad_probs - row_dot) * scale).astype(jnp.bfloat16)
        key_terms = contract(grad_scores, q_buf[:, cols], ((0,), (0,)))
        value_terms = contract(lows[h], grad_head, ((0,), (0,)))
        gk_acc[:, cols] = key_terms[:block]
        gv_acc[:, cols] = value_terms[:block]
        for level in range(levels):
            part = slice((level + 1) * block, (level + 2) * block)
            term_send[level, 0, :, cols] = key_terms[part].astype(jnp.bfloat16)
            term_send[level, 1, :, cols] = value_terms[part].astype(jnp.bfloat16)
        gq_ref[:, cols] = contract(grad_scores, k_all[:, cols], ((1,), (0,))).astype(jnp.bfloat16)

    term_copies = []
    for level in range(levels):
        term_copies.append(
            remote(
                term_send.at[level],
                term_recv.at[level],
                term_send_sem.at[level],
                term_recv_sem.at[level],
                {"seq": peer(1 << level)},
            )
        )
    for copy in term_copies:
        copy.start()

    for copy in go_copies:
        copy.wait_recv()
    for copy in att_copies:
        copy.wait_recv()
    chunks = part_send.shape[0]
    step = rows // chunks
    part_copies = []
    for i in range(chunks):
        span = slice(i * step, (i + 1) * step)
        product = contract(go_all[:, span], att_all[...], ((0,), (0,)))
        low_half, high_half = product[:, :half_w], product[:, half_w:]
        part_send[i] = jnp.where(core == 0, high_half, low_half).astype(jnp.bfloat16)
        copy = remote(
            part_send.at[i],
            part_recv.at[i],
            part_send_sem.at[i],
            part_recv_sem.at[i],
            {"fsdp": other},
        )
        copy.start()
        part_copies.append(copy)
        gw_ref[span, :] = jnp.where(core == 0, low_half, high_half)

    for copy in term_copies:
        copy.wait_recv()
    grad_key = gk_acc[...]
    grad_value = gv_acc[...]
    for level in range(levels):
        grad_key = grad_key + term_recv[level, 0].astype(jnp.float32)
        grad_value = grad_value + term_recv[level, 1].astype(jnp.float32)
    gk_ref[...] = grad_key.astype(jnp.bfloat16)
    gv_ref[...] = grad_value.astype(jnp.bfloat16)

    for i, copy in enumerate(part_copies):
        span = slice(i * step, (i + 1) * step)
        copy.wait_recv()
        gw_ref[span, :] = gw_ref[span, :] + part_recv[i].astype(jnp.float32)
    for copy in kv_copies + [w_copy] + go_copies + att_copies + term_copies + part_copies:
        copy.wait_send()


def fused_device(n_seq, query, keys, values, grad_out, w_out, link_flags):
    _, block, width = query.shape
    levels = n_seq.bit_length() - 1
    rows = D // n_seq
    chunks = 4
    shape = (block, width)
    half_w = width // 2
    vmem = pl.BlockSpec(memory_space=pltpu.VMEM)
    anywhere = pl.BlockSpec(memory_space=pl.ANY)
    bf16 = jnp.bfloat16
    dma = pltpu.SemaphoreType.DMA
    outs = pl.pallas_call(
        functools.partial(fused_kernel, n_seq),
        out_shape=[jax.ShapeDtypeStruct(shape, bf16)] * 3
        + [jax.ShapeDtypeStruct((rows, half_w), jnp.float32)],
        in_specs=[pl.BlockSpec(memory_space=pltpu.SMEM)] + [anywhere] * 5,
        out_specs=[vmem] * 4,
        scratch_shapes=[
            pltpu.VMEM(shape, bf16),
            pltpu.VMEM(((levels + 1) * block, width), bf16),
            pltpu.VMEM(((levels + 1) * block, width), bf16),
            pltpu.VMEM((block, D), bf16),
            pltpu.VMEM((2,) + w_out.shape, bf16),
            pltpu.VMEM((n_seq * block, rows), bf16),
            pltpu.VMEM((n_seq * block, width), bf16),
            pltpu.VMEM((levels, 2) + shape, bf16),
            pltpu.VMEM((levels, 2) + shape, bf16),
            pltpu.VMEM(shape, jnp.float32),
            pltpu.VMEM(shape, jnp.float32),
            pltpu.VMEM((chunks, rows // chunks, half_w), bf16),
            pltpu.VMEM((chunks, rows // chunks, half_w), bf16),
            dma((5,)),
            dma((2 * levels,)),
            dma((2 * levels,)),
            dma((2,)),
            dma((n_seq - 1,)),
            dma((n_seq - 1,)),
            dma((n_seq - 1,)),
            dma((n_seq - 1,)),
            dma((levels,)),
            dma((levels,)),
            dma((chunks,)),
            dma((chunks,)),
        ],
        compiler_params=pltpu.CompilerParams(
            collective_id=0, has_side_effects=True, vmem_limit_bytes=40 * 1024 * 1024
        ),
    )(link_flags, query[0], keys[0], values[0], grad_out[0], w_out)
    return outs[0][None], outs[1][None], outs[2][None], outs[3]


def per_device(n_seq, query, keys, values, grad_out, w_out, link_flags):
    args = (query, keys, values, grad_out, w_out, link_flags)
    if query.shape[0] == 1 and (D // n_seq) % 512 == 0 and query.shape[2] == 2 * HD:
        return fused_device(n_seq, *args)
    return plain_device(*args)


def solution(mesh):
    in_specs = (
        P("fsdp", "seq", "head"),
        P("fsdp", "seq", "head"),
        P("fsdp", "seq", "head"),
        P("fsdp", "seq", None),
        P("head", "fsdp"),
        P("seq", None),
    )
    out_specs = (
        P("fsdp", "seq", "head"),
        P("fsdp", "seq", "head"),
        P("fsdp", "seq", "head"),
        P("seq", ("head", "fsdp")),
    )
    return jax.shard_map(
        functools.partial(per_device, mesh.shape["seq"]), mesh=mesh, in_specs=in_specs, out_specs=out_specs, check_vma=False
    )
```

```python
import functools
import math

import jax
import jax.numpy as jnp
from jax import lax
from jax.experimental import pallas as pl
from jax.experimental.pallas import tpu as pltpu
from jax.sharding import PartitionSpec as P

D = 4096
HD = 128


def swapped(shard, axis, distance):
    return lax.ppermute(shard, axis, [(i, i ^ 1 << distance) for i in range(lax.axis_size(axis))])


def plain_device(query, keys, values, grad_out, w_out, link_flags):
    local_seqs, block_len, local_width = query.shape
    local_heads = local_width // HD
    levels = lax.axis_size("seq").bit_length() - 1
    score_scale = 1.0 / math.sqrt(HD)
    key_value = jnp.stack([keys, values])
    collected = [key_value]
    for level in range(levels):
        collected.append(swapped(key_value, "seq", level))
    slots = levels + 1
    near_all = jnp.stack(collected).reshape(slots, 2, local_seqs, block_len, local_heads, HD)
    key_near = near_all[:, 0]
    value_near = near_all[:, 1]
    query_heads = query.reshape(local_seqs, block_len, local_heads, HD)
    spots = jnp.arange(block_len, dtype=jnp.int32)
    causal = spots[None, :] <= spots[:, None]
    link_on = jnp.concatenate([jnp.ones((1,), dtype=bool), link_flags[0] > 0])
    first_slot = jnp.arange(slots, dtype=jnp.int32) == 0
    allowed = jnp.where(first_slot[None, :, None], causal[:, None, :], link_on[None, :, None])
    scores = (
        jnp.einsum("sthc,msuhc->shtmu", query_heads, key_near, preferred_element_type=jnp.float32)
        * score_scale
    )
    scores = jnp.where(allowed[None, None], scores, -jnp.inf)
    row_max = jnp.max(scores, axis=(3, 4), keepdims=True)
    raw = jnp.exp(scores - row_max)
    softmax = raw / jnp.sum(raw, axis=(3, 4), keepdims=True)
    probs_low = softmax.astype(jnp.bfloat16)
    attended = jnp.einsum(
        "shtmu,msuhc->sthc", probs_low, value_near, preferred_element_type=jnp.float32
    ).astype(jnp.bfloat16)
    grad_rows = grad_out.reshape(local_seqs * block_len, D)
    columns = grad_rows
    grad_att = lax.dot_general(
        columns,
        lax.all_gather(w_out, "fsdp", axis=1, tiled=True),
        (((1,), (1,)), ((), ())),
        preferred_element_type=jnp.float32,
    ).astype(jnp.bfloat16)
    grad_heads = grad_att.reshape(local_seqs, block_len, local_heads, HD)
    attended_rows = attended.reshape(local_seqs * block_len, local_width)
    columns = grad_rows
    seq_share = lax.psum_scatter(
        lax.dot_general(
            columns, attended_rows, (((0,), (0,)), ((), ())), preferred_element_type=jnp.float32
        ),
        "seq",
        scatter_dimension=0,
        tiled=True,
    )
    grad_w = lax.psum_scatter(
        seq_share.astype(jnp.bfloat16), "fsdp", scatter_dimension=1, tiled=True
    ).astype(jnp.float32)
    grad_probs = jnp.einsum(
        "sthc,msuhc->shtmu", grad_heads, value_near, preferred_element_type=jnp.float32
    )
    row_dot = jnp.sum(softmax * grad_probs, axis=(3, 4), keepdims=True)
    grad_scores = (softmax * (grad_probs - row_dot) * score_scale).astype(jnp.bfloat16)
    grad_query = jnp.einsum(
        "shtmu,msuhc->sthc", grad_scores, key_near, preferred_element_type=jnp.float32
    ).astype(jnp.bfloat16)
    key_terms = jnp.einsum(
        "shtmu,sthc->msuhc", grad_scores, query_heads, preferred_element_type=jnp.float32
    )
    value_terms = jnp.einsum(
        "shtmu,sthc->msuhc", probs_low, grad_heads, preferred_element_type=jnp.float32
    )
    grad_key = key_terms[0]
    grad_value = value_terms[0]
    for level in range(levels):
        outgoing = jnp.stack([key_terms[level + 1], value_terms[level + 1]]).astype(jnp.bfloat16)
        returned = swapped(outgoing, "seq", level)
        grad_key = grad_key + returned[0].astype(jnp.float32)
        grad_value = grad_value + returned[1].astype(jnp.float32)
    shape_out = (local_seqs, block_len, local_width)
    return (
        grad_query.reshape(shape_out),
        grad_key.astype(jnp.bfloat16).reshape(shape_out),
        grad_value.astype(jnp.bfloat16).reshape(shape_out),
        grad_w,
    )


def contract(a, b, dims):
    return lax.dot_general(a, b, (dims, ((), ())), preferred_element_type=jnp.float32)


def fused_kernel(
    n_seq,
    flags_ref,
    query_hbm,
    keys_hbm,
    values_hbm,
    go_hbm,
    w_hbm,
    gq_ref,
    gk_ref,
    gv_ref,
    gw_ref,
    q_buf,
    k_all,
    v_all,
    go_buf,
    w_all,
    go_all,
    att_all,
    term_send,
    term_recv,
    gk_acc,
    gv_acc,
    part_send,
    part_recv,
    local_sem,
    kv_send_sem,
    kv_recv_sem,
    w_sem,
    go_send_sem,
    go_recv_sem,
    pass_send_sem,
    pass_recv_sem,
    att_send_sem,
    att_recv_sem,
    term_send_sem,
    term_recv_sem,
    part_send_sem,
    part_recv_sem,
):
    levels = n_seq.bit_length() - 1
    block, width = q_buf.shape
    heads = width // HD
    rows = go_all.shape[1]
    half_d = w_hbm.shape[1]
    half_w = width // 2
    scale = 1.0 / math.sqrt(HD)
    me = lax.axis_index("seq")
    core = lax.axis_index("fsdp")
    other = 1 - core
    head = lax.axis_index("head")
    parity = head % 2
    twin = head + 1 - 2 * parity
    share = block // 2

    def peer(mask):
        out = me
        for bit in range(levels):
            if mask >> bit & 1:
                out = out + (1 << bit) * (1 - 2 * (lax.div(me, 1 << bit) % 2))
        return out

    def remote(src, dst, send, recv, target):
        return pltpu.make_async_remote_copy(
            src_ref=src,
            dst_ref=dst,
            send_sem=send,
            recv_sem=recv,
            device_id=target,
            device_id_type=pl.DeviceIdType.MESH,
        )

    locals_ = [
        pltpu.make_async_copy(query_hbm, q_buf, local_sem.at[0]),
        pltpu.make_async_copy(keys_hbm, k_all.at[pl.ds(0, block)], local_sem.at[1]),
        pltpu.make_async_copy(values_hbm, v_all.at[pl.ds(0, block)], local_sem.at[2]),
        pltpu.make_async_copy(go_hbm, go_buf, local_sem.at[3]),
        pltpu.make_async_copy(w_hbm, w_all.at[0], local_sem.at[4]),
    ]
    for copy in locals_:
        copy.start()

    barrier = pltpu.get_barrier_semaphore()
    for mask in range(1, n_seq):
        pl.semaphore_signal(
            barrier, inc=1, device_id={"seq": peer(mask)}, device_id_type=pl.DeviceIdType.MESH
        )
    pl.semaphore_signal(
        barrier, inc=1, device_id={"fsdp": other}, device_id_type=pl.DeviceIdType.MESH
    )
    pl.semaphore_signal(
        barrier, inc=1, device_id={"head": twin}, device_id_type=pl.DeviceIdType.MESH
    )
    pl.semaphore_wait(barrier, n_seq + 1)

    kv_copies = []
    for level in range(levels):
        spot = pl.ds((level + 1) * block, block)
        for which, (src, dst) in enumerate(((keys_hbm, k_all), (values_hbm, v_all))):
            i = 2 * level + which
            kv_copies.append(
                remote(
                    src,
                    dst.at[spot],
                    kv_send_sem.at[i],
                    kv_recv_sem.at[i],
                    {"seq": peer(1 << level)},
                )
            )
    for copy in kv_copies:
        copy.start()
    w_copy = remote(w_hbm, w_all.at[1], w_sem.at[0], w_sem.at[1], {"fsdp": other})
    w_copy.start()
    go_copies = []
    for mask in range(1, n_seq):
        target = peer(mask)
        columns = pl.ds(pl.multiple_of(target * rows, 128), rows)
        lines = pl.ds(pl.multiple_of(parity * share, 16), share)
        landing = pl.ds(pl.multiple_of(mask * block + parity * share, 16), share)
        go_copies.append(
            remote(
                go_hbm.at[lines, columns],
                go_all.at[landing],
                go_send_sem.at[mask - 1],
                go_recv_sem.at[mask - 1],
                {"seq": target},
            )
        )
    for copy in go_copies:
        copy.start()

    locals_[3].wait()
    locals_[4].wait()
    own_columns = pl.ds(pl.multiple_of(core * half_d, 128), half_d)
    other_columns = pl.ds(pl.multiple_of(other * half_d, 128), half_d)
    grad_att = contract(go_buf[:, own_columns], w_all[0], ((1,), (1,)))
    pass_copies = []
    for mask in range(1, n_seq):
        landing = pl.ds(pl.multiple_of(mask * block + parity * share, 16), share)
        pass_copies.append(
            remote(
                go_all.at[landing],
                go_all.at[landing],
                pass_send_sem.at[mask - 1],
                pass_recv_sem.at[mask - 1],
                {"head": twin},
            )
        )
    go_all[pl.ds(0, block), :] = go_buf[:, pl.ds(pl.multiple_of(me * rows, 128), rows)]

    for copy in locals_[:3]:
        copy.wait()
    for copy in kv_copies:
        copy.wait_recv()

    spots_t = lax.broadcasted_iota(jnp.int32, (block, block), 0)
    spots_u = lax.broadcasted_iota(jnp.int32, (block, block), 1)
    allowed = [spots_u <= spots_t]
    for level in range(levels):
        allowed.append(jnp.full((block, block), flags_ref[0, level], jnp.int32) > 0)
    allowed = jnp.concatenate(allowed, axis=1)

    softmaxes = []
    lows = []
    for h in range(heads):
        cols = slice(h * HD, (h + 1) * HD)
        scores = contract(q_buf[:, cols], k_all[:, cols], ((1,), (1,))) * scale
        scores = jnp.where(allowed, scores, -jnp.inf)
        raw = jnp.exp(scores - jnp.max(scores, axis=1, keepdims=True))
        softmax = raw / jnp.sum(raw, axis=1, keepdims=True)
        low = softmax.astype(jnp.bfloat16)
        att_all[pl.ds(0, block), cols] = contract(low, v_all[:, cols], ((1,), (0,))).astype(
            jnp.bfloat16
        )
        softmaxes.append(softmax)
        lows.append(low)

    att_copies = []
    for mask in range(1, n_seq):
        att_copies.append(
            remote(
                att_all.at[pl.ds(0, block)],
                att_all.at[pl.ds(mask * block, block)],
                att_send_sem.at[mask - 1],
                att_recv_sem.at[mask - 1],
                {"seq": peer(mask)},
            )
        )
    for copy in att_copies:
        copy.start()

    for copy, onward in zip(go_copies, pass_copies):
        copy.wait_recv()
        onward.start()
    w_copy.wait_recv()
    grad_att = grad_att + contract(go_buf[:, other_columns], w_all[1], ((1,), (1,)))
    grad_att = grad_att.astype(jnp.bfloat16)

    for h in range(heads):
        cols = slice(h * HD, (h + 1) * HD)
        grad_head = grad_att[:, cols]
        grad_probs = contract(grad_head, v_all[:, cols], ((1,), (1,)))
        row_dot = jnp.sum(softmaxes[h] * grad_probs, axis=1, keepdims=True)
        grad_scores = (softmaxes[h] * (grad_probs - row_dot) * scale).astype(jnp.bfloat16)
        key_terms = contract(grad_scores, q_buf[:, cols], ((0,), (0,)))
        value_terms = contract(lows[h], grad_head, ((0,), (0,)))
        gk_acc[:, cols] = key_terms[:block]
        gv_acc[:, cols] = value_terms[:block]
        for level in range(levels):
            part = slice((level + 1) * block, (level + 2) * block)
            term_send[level, 0, :, cols] = key_terms[part].astype(jnp.bfloat16)
            term_send[level, 1, :, cols] = value_terms[part].astype(jnp.bfloat16)
        gq_ref[:, cols] = contract(grad_scores, k_all[:, cols], ((1,), (0,))).astype(jnp.bfloat16)

    term_copies = []
    for level in range(levels):
        term_copies.append(
            remote(
                term_send.at[level],
                term_recv.at[level],
                term_send_sem.at[level],
                term_recv_sem.at[level],
                {"seq": peer(1 << level)},
            )
        )
    for copy in term_copies:
        copy.start()

    for copy in pass_copies:
        copy.wait_recv()
    for copy in att_copies:
        copy.wait_recv()
    chunks = part_send.shape[0]
    step = rows // chunks
    part_copies = []
    for i in range(chunks):
        span = slice(i * step, (i + 1) * step)
        product = contract(go_all[:, span], att_all[...], ((0,), (0,)))
        low_half, high_half = product[:, :half_w], product[:, half_w:]
        part_send[i] = jnp.where(core == 0, high_half, low_half).astype(jnp.bfloat16)
        copy = remote(
            part_send.at[i],
            part_recv.at[i],
            part_send_sem.at[i],
            part_recv_sem.at[i],
            {"fsdp": other},
        )
        copy.start()
        part_copies.append(copy)
        gw_ref[span, :] = jnp.where(core == 0, low_half, high_half)

    for copy in term_copies:
        copy.wait_recv()
    grad_key = gk_acc[...]
    grad_value = gv_acc[...]
    for level in range(levels):
        grad_key = grad_key + term_recv[level, 0].astype(jnp.float32)
        grad_value = grad_value + term_recv[level, 1].astype(jnp.float32)
    gk_ref[...] = grad_key.astype(jnp.bfloat16)
    gv_ref[...] = grad_value.astype(jnp.bfloat16)

    for i, copy in enumerate(part_copies):
        span = slice(i * step, (i + 1) * step)
        copy.wait_recv()
        gw_ref[span, :] = gw_ref[span, :] + part_recv[i].astype(jnp.float32)
    for copy in kv_copies + [w_copy] + go_copies + pass_copies + att_copies + term_copies + part_copies:
        copy.wait_send()


def deliver(*refs):
    sources, targets, sem = refs[:4], refs[4:8], refs[8]
    copies = [
        pltpu.make_async_copy(src, dst, sem.at[i]) for i, (src, dst) in enumerate(zip(sources, targets))
    ]
    for copy in copies:
        copy.start()
    for copy in copies:
        copy.wait()


def fused_device(n_seq, query, keys, values, grad_out, w_out, link_flags):
    _, block, width = query.shape
    levels = n_seq.bit_length() - 1
    rows = D // n_seq
    chunks = 4
    shape = (block, width)
    half_w = width // 2
    vmem = pl.BlockSpec(memory_space=pltpu.VMEM)
    anywhere = pl.BlockSpec(memory_space=pltpu.HBM)
    bf16 = jnp.bfloat16
    dma = pltpu.SemaphoreType.DMA
    outs = pl.pallas_call(
        functools.partial(fused_kernel, n_seq),
        out_shape=[jax.ShapeDtypeStruct(shape, bf16)] * 3
        + [jax.ShapeDtypeStruct((rows, half_w), jnp.float32)],
        in_specs=[pl.BlockSpec(memory_space=pltpu.SMEM)] + [anywhere] * 5,
        out_specs=[vmem] * 4,
        scratch_shapes=[
            pltpu.VMEM(shape, bf16),
            pltpu.VMEM(((levels + 1) * block, width), bf16),
            pltpu.VMEM(((levels + 1) * block, width), bf16),
            pltpu.VMEM((block, D), bf16),
            pltpu.VMEM((2,) + w_out.shape, bf16),
            pltpu.VMEM((n_seq * block, rows), bf16),
            pltpu.VMEM((n_seq * block, width), bf16),
            pltpu.VMEM((levels, 2) + shape, bf16),
            pltpu.VMEM((levels, 2) + shape, bf16),
            pltpu.VMEM(shape, jnp.float32),
            pltpu.VMEM(shape, jnp.float32),
            pltpu.VMEM((chunks, rows // chunks, half_w), bf16),
            pltpu.VMEM((chunks, rows // chunks, half_w), bf16),
            dma((5,)),
            dma((2 * levels,)),
            dma((2 * levels,)),
            dma((2,)),
            dma((n_seq - 1,)),
            dma((n_seq - 1,)),
            dma((n_seq - 1,)),
            dma((n_seq - 1,)),
            dma((n_seq - 1,)),
            dma((n_seq - 1,)),
            dma((levels,)),
            dma((levels,)),
            dma((chunks,)),
            dma((chunks,)),
        ],
        compiler_params=pltpu.CompilerParams(
            collective_id=0, has_side_effects=True, vmem_limit_bytes=60 * 1024 * 1024
        ),
    )(link_flags, query[0], keys[0], values[0], grad_out[0], w_out)
    outs = pl.pallas_call(
        deliver,
        out_shape=[jax.ShapeDtypeStruct(out.shape, out.dtype) for out in outs],
        in_specs=[pl.BlockSpec(memory_space=pltpu.VMEM)] * 4,
        out_specs=[pl.BlockSpec(memory_space=pltpu.HBM)] * 4,
        scratch_shapes=[dma((4,))],
    )(*outs)
    return outs[0][None], outs[1][None], outs[2][None], outs[3]


def per_device(n_seq, n_head, query, keys, values, grad_out, w_out, link_flags):
    args = (query, keys, values, grad_out, w_out, link_flags)
    if query.shape[0] == 1 and (D // n_seq) % 512 == 0 and query.shape[2] == 2 * HD and n_head % 2 == 0:
        return fused_device(n_seq, *args)
    return plain_device(*args)


def solution(mesh):
    in_specs = (
        P("fsdp", "seq", "head"),
        P("fsdp", "seq", "head"),
        P("fsdp", "seq", "head"),
        P("fsdp", "seq", None),
        P("head", "fsdp"),
        P("seq", None),
    )
    out_specs = (
        P("fsdp", "seq", "head"),
        P("fsdp", "seq", "head"),
        P("fsdp", "seq", "head"),
        P("seq", ("head", "fsdp")),
    )
    return jax.shard_map(
        functools.partial(per_device, mesh.shape["seq"], mesh.shape["head"]), mesh=mesh, in_specs=in_specs, out_specs=out_specs, check_vma=False
    )
```

```python
import functools
import math

import jax
import jax.numpy as jnp
from jax import lax
from jax.experimental import pallas as pl
from jax.experimental.pallas import tpu as pltpu
from jax.sharding import PartitionSpec as P

D = 4096
HD = 128


def swapped(shard, axis, distance):
    return lax.ppermute(shard, axis, [(i, i ^ 1 << distance) for i in range(lax.axis_size(axis))])


def plain_device(query, keys, values, grad_out, w_out, link_flags):
    local_seqs, block_len, local_width = query.shape
    local_heads = local_width // HD
    levels = lax.axis_size("seq").bit_length() - 1
    score_scale = 1.0 / math.sqrt(HD)
    key_value = jnp.stack([keys, values])
    collected = [key_value]
    for level in range(levels):
        collected.append(swapped(key_value, "seq", level))
    slots = levels + 1
    near_all = jnp.stack(collected).reshape(slots, 2, local_seqs, block_len, local_heads, HD)
    key_near = near_all[:, 0]
    value_near = near_all[:, 1]
    query_heads = query.reshape(local_seqs, block_len, local_heads, HD)
    spots = jnp.arange(block_len, dtype=jnp.int32)
    causal = spots[None, :] <= spots[:, None]
    link_on = jnp.concatenate([jnp.ones((1,), dtype=bool), link_flags[0] > 0])
    first_slot = jnp.arange(slots, dtype=jnp.int32) == 0
    allowed = jnp.where(first_slot[None, :, None], causal[:, None, :], link_on[None, :, None])
    scores = (
        jnp.einsum("sthc,msuhc->shtmu", query_heads, key_near, preferred_element_type=jnp.float32)
        * score_scale
    )
    scores = jnp.where(allowed[None, None], scores, -jnp.inf)
    row_max = jnp.max(scores, axis=(3, 4), keepdims=True)
    raw = jnp.exp(scores - row_max)
    softmax = raw / jnp.sum(raw, axis=(3, 4), keepdims=True)
    probs_low = softmax.astype(jnp.bfloat16)
    attended = jnp.einsum(
        "shtmu,msuhc->sthc", probs_low, value_near, preferred_element_type=jnp.float32
    ).astype(jnp.bfloat16)
    grad_rows = grad_out.reshape(local_seqs * block_len, D)
    columns = grad_rows
    grad_att = lax.dot_general(
        columns,
        lax.all_gather(w_out, "fsdp", axis=1, tiled=True),
        (((1,), (1,)), ((), ())),
        preferred_element_type=jnp.float32,
    ).astype(jnp.bfloat16)
    grad_heads = grad_att.reshape(local_seqs, block_len, local_heads, HD)
    attended_rows = attended.reshape(local_seqs * block_len, local_width)
    columns = grad_rows
    seq_share = lax.psum_scatter(
        lax.dot_general(
            columns, attended_rows, (((0,), (0,)), ((), ())), preferred_element_type=jnp.float32
        ),
        "seq",
        scatter_dimension=0,
        tiled=True,
    )
    grad_w = lax.psum_scatter(
        seq_share.astype(jnp.bfloat16), "fsdp", scatter_dimension=1, tiled=True
    ).astype(jnp.float32)
    grad_probs = jnp.einsum(
        "sthc,msuhc->shtmu", grad_heads, value_near, preferred_element_type=jnp.float32
    )
    row_dot = jnp.sum(softmax * grad_probs, axis=(3, 4), keepdims=True)
    grad_scores = (softmax * (grad_probs - row_dot) * score_scale).astype(jnp.bfloat16)
    grad_query = jnp.einsum(
        "shtmu,msuhc->sthc", grad_scores, key_near, preferred_element_type=jnp.float32
    ).astype(jnp.bfloat16)
    key_terms = jnp.einsum(
        "shtmu,sthc->msuhc", grad_scores, query_heads, preferred_element_type=jnp.float32
    )
    value_terms = jnp.einsum(
        "shtmu,sthc->msuhc", probs_low, grad_heads, preferred_element_type=jnp.float32
    )
    grad_key = key_terms[0]
    grad_value = value_terms[0]
    for level in range(levels):
        outgoing = jnp.stack([key_terms[level + 1], value_terms[level + 1]]).astype(jnp.bfloat16)
        returned = swapped(outgoing, "seq", level)
        grad_key = grad_key + returned[0].astype(jnp.float32)
        grad_value = grad_value + returned[1].astype(jnp.float32)
    shape_out = (local_seqs, block_len, local_width)
    return (
        grad_query.reshape(shape_out),
        grad_key.astype(jnp.bfloat16).reshape(shape_out),
        grad_value.astype(jnp.bfloat16).reshape(shape_out),
        grad_w,
    )


def contract(a, b, dims):
    return lax.dot_general(a, b, (dims, ((), ())), preferred_element_type=jnp.float32)


def fused_kernel(
    n_seq,
    flags_ref,
    query_hbm,
    keys_hbm,
    values_hbm,
    go_hbm,
    w_hbm,
    gq_out,
    gk_out,
    gv_out,
    gw_out,
    gq_ref,
    gk_ref,
    gv_ref,
    gw_ref,
    out_sem,
    q_buf,
    k_all,
    v_all,
    go_buf,
    w_all,
    go_all,
    att_all,
    term_send,
    term_recv,
    gk_acc,
    gv_acc,
    gw_acc,
    part_send,
    part_recv,
    local_sem,
    kv_send_sem,
    kv_recv_sem,
    w_sem,
    go_send_sem,
    go_recv_sem,
    pass_send_sem,
    pass_recv_sem,
    att_send_sem,
    att_recv_sem,
    term_send_sem,
    term_recv_sem,
    part_send_sem,
    part_recv_sem,
):
    levels = n_seq.bit_length() - 1
    block, width = q_buf.shape
    heads = width // HD
    rows = go_all.shape[1]
    half_d = w_hbm.shape[1]
    half_w = width // 2
    scale = 1.0 / math.sqrt(HD)
    me = lax.axis_index("seq")
    core = lax.axis_index("fsdp")
    other = 1 - core
    head = lax.axis_index("head")
    parity = head % 2
    twin = head + 1 - 2 * parity
    share = block // 2

    def peer(mask):
        out = me
        for bit in range(levels):
            if mask >> bit & 1:
                out = out + (1 << bit) * (1 - 2 * (lax.div(me, 1 << bit) % 2))
        return out

    def remote(src, dst, send, recv, target):
        return pltpu.make_async_remote_copy(
            src_ref=src,
            dst_ref=dst,
            send_sem=send,
            recv_sem=recv,
            device_id=target,
            device_id_type=pl.DeviceIdType.MESH,
        )

    locals_ = [
        pltpu.make_async_copy(query_hbm, q_buf, local_sem.at[0]),
        pltpu.make_async_copy(keys_hbm, k_all.at[pl.ds(0, block)], local_sem.at[1]),
        pltpu.make_async_copy(values_hbm, v_all.at[pl.ds(0, block)], local_sem.at[2]),
        pltpu.make_async_copy(go_hbm, go_buf, local_sem.at[3]),
        pltpu.make_async_copy(w_hbm, w_all.at[0], local_sem.at[4]),
    ]
    for copy in locals_:
        copy.start()

    barrier = pltpu.get_barrier_semaphore()
    for mask in range(1, n_seq):
        pl.semaphore_signal(
            barrier, inc=1, device_id={"seq": peer(mask)}, device_id_type=pl.DeviceIdType.MESH
        )
    pl.semaphore_signal(
        barrier, inc=1, device_id={"fsdp": other}, device_id_type=pl.DeviceIdType.MESH
    )
    pl.semaphore_signal(
        barrier, inc=1, device_id={"head": twin}, device_id_type=pl.DeviceIdType.MESH
    )
    pl.semaphore_wait(barrier, n_seq + 1)

    kv_copies = []
    for level in range(levels):
        spot = pl.ds((level + 1) * block, block)
        for which, (src, dst) in enumerate(((keys_hbm, k_all), (values_hbm, v_all))):
            i = 2 * level + which
            kv_copies.append(
                remote(
                    src,
                    dst.at[spot],
                    kv_send_sem.at[i],
                    kv_recv_sem.at[i],
                    {"seq": peer(1 << level)},
                )
            )
    for copy in kv_copies:
        copy.start()
    w_copy = remote(w_hbm, w_all.at[1], w_sem.at[0], w_sem.at[1], {"fsdp": other})
    w_copy.start()
    go_copies = []
    for mask in range(1, n_seq):
        target = peer(mask)
        columns = pl.ds(pl.multiple_of(target * rows, 128), rows)
        lines = pl.ds(pl.multiple_of(parity * share, 16), share)
        landing = pl.ds(pl.multiple_of(mask * block + parity * share, 16), share)
        go_copies.append(
            remote(
                go_hbm.at[lines, columns],
                go_all.at[landing],
                go_send_sem.at[mask - 1],
                go_recv_sem.at[mask - 1],
                {"seq": target},
            )
        )
    for copy in go_copies:
        copy.start()

    locals_[3].wait()
    locals_[4].wait()
    own_columns = pl.ds(pl.multiple_of(core * half_d, 128), half_d)
    other_columns = pl.ds(pl.multiple_of(other * half_d, 128), half_d)
    grad_att = contract(go_buf[:, own_columns], w_all[0], ((1,), (1,)))
    pass_copies = []
    for mask in range(1, n_seq):
        landing = pl.ds(pl.multiple_of(mask * block + parity * share, 16), share)
        pass_copies.append(
            remote(
                go_all.at[landing],
                go_all.at[landing],
                pass_send_sem.at[mask - 1],
                pass_recv_sem.at[mask - 1],
                {"head": twin},
            )
        )
    go_all[pl.ds(0, block), :] = go_buf[:, pl.ds(pl.multiple_of(me * rows, 128), rows)]

    for copy in locals_[:3]:
        copy.wait()
    for copy in kv_copies:
        copy.wait_recv()

    spots_t = lax.broadcasted_iota(jnp.int32, (block, block), 0)
    spots_u = lax.broadcasted_iota(jnp.int32, (block, block), 1)
    allowed = [spots_u <= spots_t]
    for level in range(levels):
        allowed.append(jnp.full((block, block), flags_ref[0, level], jnp.int32) > 0)
    allowed = jnp.concatenate(allowed, axis=1)

    softmaxes = []
    lows = []
    for h in range(heads):
        cols = slice(h * HD, (h + 1) * HD)
        scores = contract(q_buf[:, cols], k_all[:, cols], ((1,), (1,))) * scale
        scores = jnp.where(allowed, scores, -jnp.inf)
        raw = jnp.exp(scores - jnp.max(scores, axis=1, keepdims=True))
        softmax = raw / jnp.sum(raw, axis=1, keepdims=True)
        low = softmax.astype(jnp.bfloat16)
        att_all[pl.ds(0, block), cols] = contract(low, v_all[:, cols], ((1,), (0,))).astype(
            jnp.bfloat16
        )
        softmaxes.append(softmax)
        lows.append(low)

    att_copies = []
    for mask in range(1, n_seq):
        att_copies.append(
            remote(
                att_all.at[pl.ds(0, block)],
                att_all.at[pl.ds(mask * block, block)],
                att_send_sem.at[mask - 1],
                att_recv_sem.at[mask - 1],
                {"seq": peer(mask)},
            )
        )
    for copy in att_copies:
        copy.start()

    for copy, onward in zip(go_copies, pass_copies):
        copy.wait_recv()
        onward.start()
    w_copy.wait_recv()
    grad_att = grad_att + contract(go_buf[:, other_columns], w_all[1], ((1,), (1,)))
    grad_att = grad_att.astype(jnp.bfloat16)

    for h in range(heads):
        cols = slice(h * HD, (h + 1) * HD)
        grad_head = grad_att[:, cols]
        grad_probs = contract(grad_head, v_all[:, cols], ((1,), (1,)))
        row_dot = jnp.sum(softmaxes[h] * grad_probs, axis=1, keepdims=True)
        grad_scores = (softmaxes[h] * (grad_probs - row_dot) * scale).astype(jnp.bfloat16)
        key_terms = contract(grad_scores, q_buf[:, cols], ((0,), (0,)))
        value_terms = contract(lows[h], grad_head, ((0,), (0,)))
        gk_acc[:, cols] = key_terms[:block]
        gv_acc[:, cols] = value_terms[:block]
        for level in range(levels):
            part = slice((level + 1) * block, (level + 2) * block)
            term_send[level, 0, :, cols] = key_terms[part].astype(jnp.bfloat16)
            term_send[level, 1, :, cols] = value_terms[part].astype(jnp.bfloat16)
        gq_ref[:, cols] = contract(grad_scores, k_all[:, cols], ((1,), (0,))).astype(jnp.bfloat16)

    out_copies = [pltpu.make_async_copy(gq_ref, gq_out, out_sem.at[0])]
    out_copies[0].start()
    term_copies = []
    for level in range(levels):
        term_copies.append(
            remote(
                term_send.at[level],
                term_recv.at[level],
                term_send_sem.at[level],
                term_recv_sem.at[level],
                {"seq": peer(1 << level)},
            )
        )
    for copy in term_copies:
        copy.start()

    chunks = part_send.shape[0]
    step = rows // chunks
    for copy in pass_copies[:1] + att_copies[:1]:
        copy.wait_recv()
    first = slice(0, 2 * block)
    second = slice(2 * block, n_seq * block)
    for i in range(chunks):
        span = slice(i * step, (i + 1) * step)
        gw_acc[span, :] = contract(go_all[first, span], att_all[first], ((0,), (0,)))
    for copy in pass_copies[1:] + att_copies[1:]:
        copy.wait_recv()
    part_copies = []
    for i in range(chunks):
        span = slice(i * step, (i + 1) * step)
        product = gw_acc[span, :] + contract(go_all[second, span], att_all[second], ((0,), (0,)))
        low_half, high_half = product[:, :half_w], product[:, half_w:]
        part_send[i] = jnp.where(core == 0, high_half, low_half).astype(jnp.bfloat16)
        copy = remote(
            part_send.at[i],
            part_recv.at[i],
            part_send_sem.at[i],
            part_recv_sem.at[i],
            {"fsdp": other},
        )
        copy.start()
        part_copies.append(copy)
        gw_ref[span, :] = jnp.where(core == 0, low_half, high_half)

    for copy in term_copies:
        copy.wait_recv()
    grad_key = gk_acc[...]
    grad_value = gv_acc[...]
    for level in range(levels):
        grad_key = grad_key + term_recv[level, 0].astype(jnp.float32)
        grad_value = grad_value + term_recv[level, 1].astype(jnp.float32)
    gk_ref[...] = grad_key.astype(jnp.bfloat16)
    gv_ref[...] = grad_value.astype(jnp.bfloat16)
    out_copies.append(pltpu.make_async_copy(gk_ref, gk_out, out_sem.at[1]))
    out_copies.append(pltpu.make_async_copy(gv_ref, gv_out, out_sem.at[2]))
    out_copies[1].start()
    out_copies[2].start()

    for i, copy in enumerate(part_copies):
        span = slice(i * step, (i + 1) * step)
        copy.wait_recv()
        gw_ref[span, :] = gw_ref[span, :] + part_recv[i].astype(jnp.float32)
        out_copy = pltpu.make_async_copy(
            gw_ref.at[pl.ds(i * step, step)], gw_out.at[pl.ds(i * step, step)], out_sem.at[3 + i]
        )
        out_copy.start()
        out_copies.append(out_copy)
    for copy in kv_copies + [w_copy] + go_copies + pass_copies + att_copies + term_copies + part_copies:
        copy.wait_send()
    for copy in out_copies:
        copy.wait()


def deliver(*refs):
    sources, targets, sem = refs[:4], refs[4:8], refs[8]
    copies = [
        pltpu.make_async_copy(src, dst, sem.at[i]) for i, (src, dst) in enumerate(zip(sources, targets))
    ]
    for copy in copies:
        copy.start()
    for copy in copies:
        copy.wait()


def fused_device(n_seq, query, keys, values, grad_out, w_out, link_flags):
    _, block, width = query.shape
    levels = n_seq.bit_length() - 1
    rows = D // n_seq
    chunks = 2
    shape = (block, width)
    half_w = width // 2
    anywhere = pl.BlockSpec(memory_space=pltpu.HBM)
    bf16 = jnp.bfloat16
    dma = pltpu.SemaphoreType.DMA
    outs = pl.pallas_call(
        functools.partial(fused_kernel, n_seq),
        out_shape=[jax.ShapeDtypeStruct(shape, bf16)] * 3
        + [jax.ShapeDtypeStruct((rows, half_w), jnp.float32)],
        in_specs=[pl.BlockSpec(memory_space=pltpu.SMEM)] + [anywhere] * 5,
        out_specs=[pl.BlockSpec(memory_space=pltpu.HBM)] * 4,
        scratch_shapes=[
            pltpu.VMEM(shape, bf16),
            pltpu.VMEM(shape, bf16),
            pltpu.VMEM(shape, bf16),
            pltpu.VMEM((rows, half_w), jnp.float32),
            dma((3 + chunks,)),
            pltpu.VMEM(shape, bf16),
            pltpu.VMEM(((levels + 1) * block, width), bf16),
            pltpu.VMEM(((levels + 1) * block, width), bf16),
            pltpu.VMEM((block, D), bf16),
            pltpu.VMEM((2,) + w_out.shape, bf16),
            pltpu.VMEM((n_seq * block, rows), bf16),
            pltpu.VMEM((n_seq * block, width), bf16),
            pltpu.VMEM((levels, 2) + shape, bf16),
            pltpu.VMEM((levels, 2) + shape, bf16),
            pltpu.VMEM(shape, jnp.float32),
            pltpu.VMEM(shape, jnp.float32),
            pltpu.VMEM((rows, width), jnp.float32),
            pltpu.VMEM((chunks, rows // chunks, half_w), bf16),
            pltpu.VMEM((chunks, rows // chunks, half_w), bf16),
            dma((5,)),
            dma((2 * levels,)),
            dma((2 * levels,)),
            dma((2,)),
            dma((n_seq - 1,)),
            dma((n_seq - 1,)),
            dma((n_seq - 1,)),
            dma((n_seq - 1,)),
            dma((n_seq - 1,)),
            dma((n_seq - 1,)),
            dma((levels,)),
            dma((levels,)),
            dma((chunks,)),
            dma((chunks,)),
        ],
        compiler_params=pltpu.CompilerParams(
            collective_id=0, has_side_effects=True, vmem_limit_bytes=60 * 1024 * 1024
        ),
    )(link_flags, query[0], keys[0], values[0], grad_out[0], w_out)
    outs = pl.pallas_call(
        deliver,
        out_shape=[jax.ShapeDtypeStruct(out.shape, out.dtype) for out in outs],
        in_specs=[pl.BlockSpec(memory_space=pltpu.VMEM)] * 4,
        out_specs=[pl.BlockSpec(memory_space=pltpu.HBM)] * 4,
        scratch_shapes=[dma((4,))],
    )(*outs)
    return outs[0][None], outs[1][None], outs[2][None], outs[3]


def per_device(n_seq, n_head, query, keys, values, grad_out, w_out, link_flags):
    args = (query, keys, values, grad_out, w_out, link_flags)
    if query.shape[0] == 1 and (D // n_seq) % 512 == 0 and query.shape[2] == 2 * HD and n_head % 2 == 0:
        return fused_device(n_seq, *args)
    return plain_device(*args)


def solution(mesh):
    in_specs = (
        P("fsdp", "seq", "head"),
        P("fsdp", "seq", "head"),
        P("fsdp", "seq", "head"),
        P("fsdp", "seq", None),
        P("head", "fsdp"),
        P("seq", None),
    )
    out_specs = (
        P("fsdp", "seq", "head"),
        P("fsdp", "seq", "head"),
        P("fsdp", "seq", "head"),
        P("seq", ("head", "fsdp")),
    )
    return jax.shard_map(
        functools.partial(per_device, mesh.shape["seq"], mesh.shape["head"]), mesh=mesh, in_specs=in_specs, out_specs=out_specs, check_vma=False
    )
```
